32 devices in a mesh: section: 4 (over y, x), adapter: 2 (over core), mp: 4 (over z).
Axes of the slice: x: 2, y: 2, z: 4, core: 2. Of those that a mesh axis runs over, the one named last changes fastest.
Arguments:
- forward_input: bfloat16 [4, 2048, 8192], P('section', 'adapter', 'mp'), may hold values from -6 to 6
- stored_input: bfloat16 [4, 2048, 8192], P('section', 'adapter', 'mp'), may hold values from -6 to 6
- output_gradient: bfloat16 [4, 2048, 8192], P('section', 'adapter', 'mp'), may hold values from -6 to 6
- frozen_weight: bfloat16 [4, 8192, 8192], P('section', None, 'mp'), may hold values from -0.0625 to 0.0625
- adapter_down_factor: bfloat16 [4, 16, 64, 8192], P('section', 'adapter', None, 'mp'), may hold values from -0.0625 to 0.0625
- adapter_up_factor: bfloat16 [4, 16, 64, 8192], P('section', 'adapter', None, 'mp'), may hold values from -0.0625 to 0.0625
- adapter_index_list: int32 [2, 4, 16], P(None, 'section', 'adapter'), may hold values from 0 to 15, as said below
Outputs:
- fwd_out: bfloat16 [4, 2048, 8192], P('section', 'adapter', 'mp')
- grad_in: bfloat16 [4, 2048, 8192], P('section', 'adapter', 'mp')
- grad_a: bfloat16 [4, 16, 64, 8192], P('section', 'adapter', None, 'mp')
- grad_b: bfloat16 [4, 16, 64, 8192], P('section', 'adapter', None, 'mp')
The draws below stay inside these ranges and needn't reach their ends.
Inputs may be any that keep to these rules, and one draw needn't show every extreme that they name: `adapter_index_list`: owner o holds adapters o * 8 to (o + 1) * 8 - 1. Of the 8 sequences of one index of the adapter axis, for one segment and one micro-batch, at most 5 use adapters of one owner; for each segment and micro-batch one owner gets exactly 5 from every index.
All inputs are finite; a program needn't handle non-finite values.
Results may differ from the reference program's by a relative error of at most 0.013.
Values may be sent and summed in bfloat16 or wider, within the bound.
A program may use at most 192 MiB of HBM per device.

```python
import jax
import jax.numpy as jnp
from jax import lax

MODEL_WIDTH = 8192
ADAPTER_RANK = 64
SEQ_LEN = 128
SEQ_DEV = 8
ADP_DEV = 8
RELAY_SEGMENTS = 4
SEGMENT_ADAPTERS = 16
SEQS = 16
MICRO_TOKENS = 2048
CAP = 5
N_MP = 4


def draw_adapter_index_list(key, part):
    owners_count = SEQS // SEQ_DEV
    slot_total = owners_count * CAP
    key_hot, key_rest = jax.random.split(key)
    hot_owner = jax.random.randint(key_hot, (2 * RELAY_SEGMENTS,), 0, owners_count)
    hot_each = jnp.repeat(hot_owner, owners_count)
    block_keys = jax.random.split(key_rest, 2 * RELAY_SEGMENTS * owners_count)

    def one_block(block_key, hot_one):
        key_score, key_shuffle, key_local = jax.random.split(block_key, 3)
        raw_score = jax.random.randint(key_score, (slot_total,), 0, 1 << 20)
        slot_ids = jnp.arange(slot_total, dtype=jnp.int32)
        scores = raw_score * slot_total + slot_ids + jnp.where(slot_ids // CAP == hot_one, 1 << 30, 0)
        top_values, chosen = lax.top_k(scores, SEQ_DEV)
        owners = (chosen // CAP).astype(jnp.int32)
        shuffle = jax.random.permutation(key_shuffle, SEQ_DEV)
        owners = owners[shuffle]
        local_ids = jax.random.randint(key_local, (SEQ_DEV,), 0, ADP_DEV)
        return owners * ADP_DEV + local_ids
    blocks_drawn = jax.vmap(one_block)(block_keys, hot_each)
    return blocks_drawn.reshape(2, RELAY_SEGMENTS, SEQS).astype(jnp.int32)


def block_levels(rng, dims, cuts, least, largest):
    def one(axis_at, blocks):
        heights = jax.random.uniform(jax.random.fold_in(jax.random.fold_in(rng, 6), axis_at), (blocks,), jnp.float32, least / len(cuts), largest / len(cuts))
        return jnp.repeat(jnp.exp(heights), dims[axis_at] // blocks).reshape((-1,) + (1,) * (len(dims) - axis_at - 1))

    loudness = one(*cuts[0])
    for cut in cuts[1:]:
        loudness = loudness * one(*cut)
    return loudness


def normal_values(own_key, dims, spread, limit, cuts=(), kind=jnp.bfloat16):
    array = spread * jax.random.normal(own_key, dims, jnp.float32)
    if cuts:
        array = array * block_levels(own_key, dims, cuts, -0.22, 0.18)
    return jnp.clip(array, -limit, limit).astype(kind)


def setup_inputs(seed: int = 0) -> dict:
    arg_keys = jax.random.split(jax.random.key(seed), 8)
    forward_input = normal_values(arg_keys[0], (RELAY_SEGMENTS, MICRO_TOKENS, MODEL_WIDTH), 1.0, 6.0, ((0, 4), (1, 2), (2, 4)))
    stored_input = normal_values(arg_keys[1], (RELAY_SEGMENTS, MICRO_TOKENS, MODEL_WIDTH), 1.0, 6.0, ((0, 4), (1, 2), (2, 4)))
    output_gradient = normal_values(arg_keys[2], (RELAY_SEGMENTS, MICRO_TOKENS, MODEL_WIDTH), 1.0, 6.0, ((0, 4), (1, 2), (2, 4)))
    frozen_weight = normal_values(arg_keys[3], (RELAY_SEGMENTS, MODEL_WIDTH, MODEL_WIDTH), MODEL_WIDTH ** -0.5, 0.0625, ((0, 4), (2, 4)))
    adapter_down_factor = normal_values(arg_keys[4], (RELAY_SEGMENTS, SEGMENT_ADAPTERS, ADAPTER_RANK, MODEL_WIDTH), MODEL_WIDTH ** -0.5, 0.0625, ((0, 4), (1, 2), (3, 4)))
    adapter_up_factor = normal_values(arg_keys[5], (RELAY_SEGMENTS, SEGMENT_ADAPTERS, ADAPTER_RANK, MODEL_WIDTH), MODEL_WIDTH ** -0.5, 0.0625, ((0, 4), (1, 2), (3, 4)))
    adapter_index_list = draw_adapter_index_list(jax.random.fold_in(arg_keys[7], 71), 0)
    return {"forward_input": forward_input, "stored_input": stored_input, "output_gradient": output_gradient, "frozen_weight": frozen_weight, "adapter_down_factor": adapter_down_factor, "adapter_up_factor": adapter_up_factor, "adapter_index_list": adapter_index_list}


adapter_scale = 2.0


def reference(forward_input, stored_input, output_gradient, frozen_weight, adapter_down_factor, adapter_up_factor, adapter_index_list):
    single_float = jnp.float32
    brain_half_float = jnp.bfloat16
    highest_accuracy = lax.Precision.HIGHEST
    width_part = MODEL_WIDTH // N_MP
    fwd_list = []
    back_list = []
    grad_a_list = []
    grad_b_list = []
    for relay_segment_index in range(RELAY_SEGMENTS):
        hidden_state = forward_input[relay_segment_index]
        weight = frozen_weight[relay_segment_index]
        down_factor_table = adapter_down_factor[relay_segment_index]
        up_factor_table = adapter_up_factor[relay_segment_index]
        forward_adapter_index = adapter_index_list[0, relay_segment_index]
        ids_back = adapter_index_list[1, relay_segment_index]
        frozen_base = jnp.dot(hidden_state, weight, preferred_element_type=single_float)
        rows_fwd = hidden_state.reshape(SEQS, SEQ_LEN, MODEL_WIDTH).astype(single_float)
        encoded_rows = jnp.einsum('msg,mog->mos', rows_fwd, down_factor_table[forward_adapter_index].astype(single_float), precision=highest_accuracy).astype(brain_half_float)
        adapter_token_rows = jnp.einsum('zpe,zpc->zec', encoded_rows.astype(single_float), up_factor_table[forward_adapter_index].astype(single_float), precision=highest_accuracy).astype(brain_half_float)
        forward_output = hidden_state.astype(single_float) + frozen_base + adapter_scale * adapter_token_rows.astype(single_float).reshape(MICRO_TOKENS, MODEL_WIDTH)
        fwd_list.append(forward_output.astype(brain_half_float))

        saved = stored_input[relay_segment_index]
        cotangent = output_gradient[relay_segment_index]
        first_sel = down_factor_table[ids_back].astype(single_float)
        second_selection = up_factor_table[ids_back].astype(single_float)
        rows_saved = saved.reshape(SEQS, SEQ_LEN, MODEL_WIDTH).astype(single_float)
        token_row_gradient = cotangent.reshape(SEQS, SEQ_LEN, MODEL_WIDTH).astype(single_float)
        encoded_backward = jnp.einsum('msg,mog->mos', rows_saved, first_sel, precision=highest_accuracy).astype(brain_half_float)
        gradient_scaled = (adapter_scale * jnp.einsum('msg,mog->mos', token_row_gradient, second_selection, precision=highest_accuracy)).astype(brain_half_float)
        back_rows = jnp.einsum('zpe,zpc->zec', gradient_scaled.astype(single_float), first_sel, precision=highest_accuracy).astype(brain_half_float)
        back_sum = jnp.zeros((MICRO_TOKENS, MODEL_WIDTH), single_float)
        for mp_index in range(N_MP):
            columns_g = cotangent[:, mp_index * width_part:(mp_index + 1) * width_part]
            columns_w = weight[:, mp_index * width_part:(mp_index + 1) * width_part]
            partial_term = lax.dot_general(columns_g, columns_w, (((1,), (1,)), ((), ())), preferred_element_type=single_float)
            back_sum = back_sum + partial_term.astype(brain_half_float).astype(single_float)
        out_back = cotangent.astype(single_float) + back_sum + back_rows.astype(single_float).reshape(MICRO_TOKENS, MODEL_WIDTH)
        back_list.append(out_back.astype(brain_half_float))

        per_seq_a = jnp.einsum('vic,vcw->viw', gradient_scaled.astype(single_float), rows_saved, precision=highest_accuracy)
        sequence_up_factor = adapter_scale * jnp.einsum('vic,vcw->viw', encoded_backward.astype(single_float), token_row_gradient, precision=highest_accuracy)
        onehot = (ids_back[:, None] == jnp.arange(SEGMENT_ADAPTERS, dtype=jnp.int32)[None, :]).astype(single_float)
        grad_a_list.append((jnp.einsum('qj,qrd->jrd', onehot, per_seq_a, precision=highest_accuracy) / SEQ_LEN).astype(brain_half_float))
        grad_b_list.append((jnp.einsum('qj,qrd->jrd', onehot, sequence_up_factor, precision=highest_accuracy) / SEQ_LEN).astype(brain_half_float))
    fwd_out = jnp.roll(jnp.stack(fwd_list), 1, axis=0)
    grad_in = jnp.roll(jnp.stack(back_list), -1, axis=0)
    return (fwd_out, grad_in, jnp.stack(grad_a_list), jnp.stack(grad_b_list))
```

```python
import jax
import jax.numpy as jnp
from jax import lax
from jax.sharding import PartitionSpec as P

adapter_scale = 2.0
chunk_count = 2
longest_line = 4


def shifted(value, axis, steps):
    count = lax.axis_size(axis)
    pairs = [(source, (source + steps) % count) for source in range(count)]
    return lax.ppermute(value, axis, pairs)


def line_gather(block, axis):
    n = lax.axis_size(axis)
    me = lax.axis_index(axis)
    up, down = [block], [block]
    for t in range(1, n):
        up.append(lax.ppermute(up[-1], axis, [(j, j + 1) for j in range(t - 1, n - 1)]))
        down.append(lax.ppermute(down[-1], axis, [(j, j - 1) for j in range(1, n - t + 1)]))
    return [block] + [jnp.where(me + k < n, down[k], up[n - k]) for k in range(1, n)]


def line_scatter(terms, axis):
    n = lax.axis_size(axis)
    up = down = None
    for t in range(1, n):
        first, second = terms[n - t], terms[t]
        if up is not None:
            first = (first.astype(jnp.float32) + up.astype(jnp.float32)).astype(jnp.bfloat16)
            second = (second.astype(jnp.float32) + down.astype(jnp.float32)).astype(jnp.bfloat16)
        up = lax.ppermute(first, axis, [(j, j + 1) for j in range(t)])
        down = lax.ppermute(second, axis, [(j, j - 1) for j in range(n - t, n)])
    return terms[0].astype(jnp.float32) + up.astype(jnp.float32) + down.astype(jnp.float32)


def summed(value, axis):
    n = lax.axis_size(axis)
    if n > longest_line or n & (n - 1):
        return lax.psum(value, axis)
    step = 1
    while step < n:
        pairs = [(j, j ^ step) for j in range(n)]
        other = lax.ppermute(value.astype(jnp.bfloat16), axis, pairs)
        value = value + other.astype(jnp.float32)
        step *= 2
    return value


def dot(a, b, a_dim=1, b_dim=0):
    return lax.dot_general(
        a, b, (((a_dim,), (b_dim,)), ((), ())), preferred_element_type=jnp.float32
    )


def local(
    forward_input,
    stored_input,
    output_gradient,
    frozen_weight,
    adapter_down_factor,
    adapter_up_factor,
    adapter_index_list,
):
    f32, bf16 = jnp.float32, jnp.bfloat16
    h, x, g = forward_input[0], stored_input[0], output_gradient[0]
    weight = frozen_weight[0]
    n = lax.axis_size("mp")
    me = lax.axis_index("mp")
    owners = lax.axis_size("adapter")
    core = lax.axis_index("adapter")
    held, rank, width = adapter_down_factor.shape[1:]
    rows = h.shape[0]
    seq_count = adapter_index_list.shape[2]
    seq_len = rows // seq_count
    part = rows // chunk_count
    line = n <= longest_line

    def pieces(value):
        return [value[c * part : (c + 1) * part] for c in range(chunk_count)]

    h_parts, g_parts = pieces(h), pieces(g)

    if line:
        w_blocks = [
            lax.dynamic_slice_in_dim(weight, ((me + k) % n) * width, width, 0) for k in range(n)
        ]
        gathered = [line_gather(piece, "mp") for piece in h_parts]
        back_sums = []
        for piece in g_parts:
            terms = [None] * n
            order = [k for t in range(1, n) for k in (n - t, t)] + [0]
            for k in order:
                if terms[k] is None:
                    terms[k] = dot(piece, w_blocks[k], 1, 1).astype(bf16)
            back_sums.append(line_scatter(terms, "mp"))
        bases = []
        for blocks in gathered:
            base = dot(blocks[0], w_blocks[0])
            for k in range(1, n):
                base = base + dot(blocks[k], w_blocks[k])
            bases.append(base)
    else:
        bases = [
            dot(lax.all_gather(piece, "mp", axis=1, tiled=True), weight) for piece in h_parts
        ]
        back_sums = [
            lax.psum_scatter(
                dot(piece, weight, 1, 1).astype(bf16), "mp", scatter_dimension=1, tiled=True
            ).astype(f32)
            for piece in g_parts
        ]

    def all_tables(table):
        flat = table.reshape(held * rank, width)
        return jnp.concatenate(
            [flat] + [shifted(flat, "adapter", -k) for k in range(1, owners)], axis=0
        )

    down_all = all_tables(adapter_down_factor[0])
    up_all = all_tables(adapter_up_factor[0])
    total = owners * held
    columns = total * rank

    def mask_of(ids):
        place = (ids - core * held + total) % total
        token_place = jnp.repeat(place, seq_len)
        owner = lax.broadcasted_iota(jnp.int32, (rows, columns), 1) // rank
        return token_place[:, None] == owner

    mask_fwd = mask_of(adapter_index_list[0, 0])
    mask_back = mask_of(adapter_index_list[1, 0])
    fold = (
        lax.broadcasted_iota(jnp.int32, (columns, rank), 0) % rank
        == lax.broadcasted_iota(jnp.int32, (columns, rank), 1)
    ).astype(bf16)

    def rank_product(values, table, mask):
        product = jnp.where(mask, dot(values, table, 1, 1), 0.0).astype(bf16)
        return dot(fold, product, 0, 1)

    def spread(code, mask):
        return jnp.where(mask, dot(code, fold, 0, 1), 0.0).astype(bf16)

    ranked = jnp.concatenate(
        [
            rank_product(h, down_all, mask_fwd),
            rank_product(x, down_all, mask_back),
            rank_product(g, up_all, mask_back),
        ],
        axis=1,
    )
    ranked = summed(ranked, "mp")
    u = spread(ranked[:, :rows].astype(bf16), mask_fwd)
    ub = spread(ranked[:, rows : 2 * rows].astype(bf16), mask_back)
    v = spread((adapter_scale * ranked[:, 2 * rows :]).astype(bf16), mask_back)

    def factor_gradient(code, values, scale):
        own = dot(code[:, : held * rank], values, 0, 0)
        for k in range(1, owners):
            theirs = dot(code[:, k * held * rank : (k + 1) * held * rank], values, 0, 0)
            own = own + shifted(theirs.astype(bf16), "adapter", k).astype(f32)
        return (own * scale).astype(bf16).reshape(held, rank, width)

    grad_a = factor_gradient(v, x, 1.0 / seq_len)
    grad_b = factor_gradient(ub, g, adapter_scale / seq_len)

    fwd_next, back_next = [], []
    for c, (u_part, v_part) in enumerate(zip(pieces(u), pieces(v))):
        lora = dot(u_part, up_all).astype(bf16).astype(f32)
        out = h_parts[c].astype(f32) + bases[c] + adapter_scale * lora
        fwd_next.append(shifted(out.astype(bf16), "section", 1))
        w = dot(v_part, down_all).astype(bf16).astype(f32)
        out = g_parts[c].astype(f32) + back_sums[c] + w
        back_next.append(shifted(out.astype(bf16), "section", -1))
    fwd_next = jnp.concatenate(fwd_next, axis=0)
    back_next = jnp.concatenate(back_next, axis=0)
    return (fwd_next[None], back_next[None], grad_a[None], grad_b[None])


def solution(mesh):
    in_specs = (
        P("section", "adapter", "mp"),
        P("section", "adapter", "mp"),
        P("section", "adapter", "mp"),
        P("section", None, "mp"),
        P("section", "adapter", None, "mp"),
        P("section", "adapter", None, "mp"),
        P(None, "section", "adapter"),
    )
    out_specs = (
        P("section", "adapter", "mp"),
        P("section", "adapter", "mp"),
        P("section", "adapter", None, "mp"),
        P("section", "adapter", None, "mp"),
    )
    return jax.shard_map(local, mesh=mesh, in_specs=in_specs, out_specs=out_specs, check_vma=False)
```

```python
import functools

import jax
import jax.numpy as jnp
from jax import lax
from jax.experimental import pallas as pl
from jax.experimental.pallas import tpu as pltpu
from jax.sharding import PartitionSpec as P

adapter_scale = 2.0
chunk_count = 4
longest_line = 4


def shifted(value, axis, steps):
    count = lax.axis_size(axis)
    pairs = [(source, (source + steps) % count) for source in range(count)]
    return lax.ppermute(value, axis, pairs)


def relay_kernel(
    n, chunks, h, g, weight, fwd_add, back_add,
    fwd_next, back_next, blocks, arrived, sending, results,
    gather_send, gather_recv, sum_send, sum_recv, relay_send, relay_recv, own_sem,
):
    me = lax.axis_index("mp")
    section = lax.axis_index("section")
    sections = lax.axis_size("section")
    after = lax.rem(section + 1, sections)
    before = lax.rem(section + sections - 1, sections)
    rows, width = h.shape
    part = rows // chunks
    tile = min(512, width)
    narrow = min(256, width)
    mesh_id = pl.DeviceIdType.MESH

    def here(c):
        return pl.ds(pl.multiple_of(c * part, part), part)

    barrier = pltpu.get_barrier_semaphore()
    for other in (after, before):
        pl.semaphore_signal(barrier, 1, device_id={"section": other}, device_id_type=mesh_id)

    @pl.when(me > 0)
    def _():
        pl.semaphore_signal(barrier, 1, device_id={"mp": me - 1}, device_id_type=mesh_id)

    @pl.when(me < n - 1)
    def _():
        pl.semaphore_signal(barrier, 1, device_id={"mp": me + 1}, device_id_type=mesh_id)

    pl.semaphore_wait(barrier, 2 + (me > 0).astype(jnp.int32) + (me < n - 1).astype(jnp.int32))

    own = pltpu.make_async_copy(h, blocks.at[me], own_sem)
    own.start()

    def position(way):
        return me + way * (n - 1 - 2 * me)

    def toward(way):
        return me + 1 - 2 * way

    def gather_copy(way, t, c):
        block = me - (1 - 2 * way) * (t - 1)
        return pltpu.make_async_remote_copy(
            src_ref=h.at[here(c)] if isinstance(t, int) and t == 1 else blocks.at[block, here(c)],
            dst_ref=blocks.at[block, here(c)],
            send_sem=gather_send.at[way, t, c],
            recv_sem=gather_recv.at[way, t, c],
            device_id={"mp": toward(way)},
            device_id_type=mesh_id,
        )

    def gather_wait(way, t, c):
        block = me - (1 - 2 * way) * t
        pltpu.make_async_copy(
            blocks.at[block, here(c)], blocks.at[block, here(c)], gather_recv.at[way, t, c]
        ).wait()

    def sum_copy(way, t, c):
        block = me + (1 - 2 * way) * (n - t)
        return pltpu.make_async_remote_copy(
            src_ref=sending.at[block, here(c)],
            dst_ref=arrived.at[way, t, here(c)],
            send_sem=sum_send.at[way, t, c],
            recv_sem=sum_recv.at[way, t, c],
            device_id={"mp": toward(way)},
            device_id_type=mesh_id,
        )

    def sum_wait(way, t, c):
        pltpu.make_async_copy(
            arrived.at[way, t, here(c)], arrived.at[way, t, here(c)], sum_recv.at[way, t, c]
        ).wait()

    def relay_copy(which, c):
        return pltpu.make_async_remote_copy(
            src_ref=results.at[which, here(c)],
            dst_ref=(fwd_next, back_next)[which].at[here(c)],
            send_sem=relay_send.at[which, c],
            recv_sem=relay_recv.at[which, c],
            device_id={"section": (after, before)[which]},
            device_id_type=mesh_id,
        )

    def weight_rows(block):
        return weight.at[pl.ds(pl.multiple_of(block * width, width), width)]

    def product(block, c):
        return (
            [
                pl.BlockSpec((part, width), lambda j: (0, 0)),
                pl.BlockSpec((tile, width), lambda j: (j, 0)),
            ],
            [g.at[here(c)], weight_rows(block)],
        )

    piece = pl.BlockSpec((part, tile), lambda j: (0, j))

    def first_sum(block, c):
        def body(g_ref, w_ref, out_ref):
            out_ref[...] = dot(g_ref[...], w_ref[...], 1, 1).astype(jnp.bfloat16)

        specs, refs = product(block, c)
        pltpu.emit_pipeline(
            body, grid=(width // tile,), in_specs=specs, out_specs=[piece]
        )(*refs, sending.at[block, here(c)])

    def later_sum(way, t, block, c):
        def body(g_ref, w_ref, old_ref, out_ref):
            term = dot(g_ref[...], w_ref[...], 1, 1)
            out_ref[...] = (term + old_ref[...].astype(jnp.float32)).astype(jnp.bfloat16)

        specs, refs = product(block, c)
        pltpu.emit_pipeline(
            body, grid=(width // tile,), in_specs=specs + [piece], out_specs=[piece]
        )(*refs, arrived.at[way, t - 1, here(c)], sending.at[block, here(c)])

    def last_sum(c):
        def body(g_ref, w_ref, up_ref, down_ref, add_ref, out_ref):
            total = dot(g_ref[...], w_ref[...], 1, 1) + add_ref[...]
            up = jnp.where(me > 0, up_ref[...].astype(jnp.float32), 0.0)
            down = jnp.where(me < n - 1, down_ref[...].astype(jnp.float32), 0.0)
            out_ref[...] = (total + up + down).astype(jnp.bfloat16)

        specs, refs = product(me, c)
        pltpu.emit_pipeline(
            body, grid=(width // tile,), in_specs=specs + [piece] * 3, out_specs=[piece]
        )(
            *refs,
            arrived.at[0, n - 1, here(c)],
            arrived.at[1, n - 1, here(c)],
            back_add.at[here(c)],
            results.at[1, here(c)],
        )

    def base(c):
        def body(b_ref, w_ref, add_ref, out_ref):
            total = add_ref[...]
            for k in range(n):
                total = total + dot(b_ref[k], w_ref[k * width : (k + 1) * width, :])
            out_ref[...] = total.astype(jnp.bfloat16)

        strip = pl.BlockSpec((part, narrow), lambda j: (0, j))
        pltpu.emit_pipeline(
            body,
            grid=(width // narrow,),
            in_specs=[
                pl.BlockSpec((n, part, width), lambda j: (0, 0, 0)),
                pl.BlockSpec((n * width, narrow), lambda j: (0, j)),
                strip,
            ],
            out_specs=[strip],
        )(blocks.at[:, here(c)], weight, fwd_add.at[here(c)], results.at[0, here(c)])

    def start_gather(c):
        for way in range(2):
            @pl.when((c < chunks) & (position(way) < n - 1))
            def _():
                gather_copy(way, 1, c).start()

    start_gather(0)

    @pl.loop(0, chunks + n - 1)
    def _(slot):
        start_gather(slot + 1)

        @pl.loop(1, n)
        def _(t):
            c = slot - t + 1

            @pl.loop(0, 2)
            def _(way):
                place = position(way)

                @pl.when((c >= 0) & (c < chunks) & (place <= t - 1))
                def _():
                    block = me + (1 - 2 * way) * (n - t)

                    @pl.when(place == 0)
                    def _():
                        first_sum(block, c)

                    @pl.when(place > 0)
                    def _():
                        sum_wait(way, t - 1, c)
                        later_sum(way, t, block, c)

                    sum_copy(way, t, c).start()

                d = slot - t

                @pl.when((d >= 0) & (d < chunks) & (place >= t))
                def _():
                    gather_wait(way, t, d)

                    @pl.when(place < n - 1)
                    def _():
                        gather_copy(way, t + 1, d).start()

        done = slot - (n - 1)

        @pl.when(done == 0)
        def _():
            own.wait()

        @pl.when(done >= 0)
        def _():
            base(done)
            relay_copy(0, done).start()
            for way in range(2):
                @pl.when(position(way) > 0)
                def _():
                    sum_wait(way, n - 1, done)
            last_sum(done)
            relay_copy(1, done).start()

    @pl.loop(0, chunks)
    def _(c):
        for way in range(2):
            @pl.when(position(way) < n - 1)
            def _():
                gather_copy(way, 1, c).wait_send()

            @pl.loop(1, n)
            def _(t):
                @pl.when((position(way) < n - 1) & (position(way) >= t - 1) & (t > 1))
                def _():
                    gather_copy(way, t, c).wait_send()

                @pl.when(position(way) <= t - 1)
                def _():
                    sum_copy(way, t, c).wait_send()
            relay_copy(way, c).wait_send()
            relay_copy(way, c).wait_recv()


def relay(h, g, weight, fwd_add, back_add, chunks):
    n = lax.axis_size("mp")
    rows, width = h.shape
    part = (rows, width)
    shapes = [part, part, (n,) + part, (2, n) + part, (n,) + part, (2,) + part]
    anywhere = pl.BlockSpec(memory_space=pl.ANY)
    dma = pltpu.SemaphoreType.DMA
    work = rows * weight.shape[0] * width * 4
    return pl.pallas_call(
        functools.partial(relay_kernel, n, chunks),
        out_shape=[jax.ShapeDtypeStruct(shape, jnp.bfloat16) for shape in shapes],
        in_specs=[anywhere] * 5,
        out_specs=[anywhere] * 6,
        scratch_shapes=[
            dma((2, n, chunks)), dma((2, n, chunks)),
            dma((2, n, chunks)), dma((2, n, chunks)),
            dma((2, chunks)), dma((2, chunks)), dma,
        ],
        compiler_params=pltpu.CompilerParams(
            collective_id=0, has_side_effects=True, vmem_limit_bytes=48 * 2**20
        ),
        cost_estimate=pl.CostEstimate(flops=work, bytes_accessed=10**9, transcendentals=0),
    )(h, g, weight, fwd_add, back_add)[:2]


def summed(value, axis):
    n = lax.axis_size(axis)
    if n > longest_line or n & (n - 1):
        return lax.psum(value, axis)
    step = 1
    while step < n:
        pairs = [(j, j ^ step) for j in range(n)]
        other = lax.ppermute(value.astype(jnp.bfloat16), axis, pairs)
        value = value + other.astype(jnp.float32)
        step *= 2
    return value


def dot(a, b, a_dim=1, b_dim=0):
    return lax.dot_general(
        a, b, (((a_dim,), (b_dim,)), ((), ())), preferred_element_type=jnp.float32
    )


def local(
    forward_input,
    stored_input,
    output_gradient,
    frozen_weight,
    adapter_down_factor,
    adapter_up_factor,
    adapter_index_list,
):
    f32, bf16 = jnp.float32, jnp.bfloat16
    h, x, g = forward_input[0], stored_input[0], output_gradient[0]
    weight = frozen_weight[0]
    n = lax.axis_size("mp")
    owners = lax.axis_size("adapter")
    core = lax.axis_index("adapter")
    held, rank, width = adapter_down_factor.shape[1:]
    rows = h.shape[0]
    seq_count = adapter_index_list.shape[2]
    seq_len = rows // seq_count
    def all_tables(table):
        flat = table.reshape(held * rank, width)
        return jnp.concatenate(
            [flat] + [shifted(flat, "adapter", -k) for k in range(1, owners)], axis=0
        )

    down_all = all_tables(adapter_down_factor[0])
    up_all = all_tables(adapter_up_factor[0])
    total = owners * held
    columns = total * rank

    def mask_of(ids):
        place = (ids - core * held + total) % total
        token_place = jnp.repeat(place, seq_len)
        owner = lax.broadcasted_iota(jnp.int32, (rows, columns), 1) // rank
        return token_place[:, None] == owner

    mask_fwd = mask_of(adapter_index_list[0, 0])
    mask_back = mask_of(adapter_index_list[1, 0])
    fold = (
        lax.broadcasted_iota(jnp.int32, (columns, rank), 0) % rank
        == lax.broadcasted_iota(jnp.int32, (columns, rank), 1)
    ).astype(bf16)

    def rank_product(values, table, mask):
        product = jnp.where(mask, dot(values, table, 1, 1), 0.0).astype(bf16)
        return dot(fold, product, 0, 1)

    def spread(code, mask):
        return jnp.where(mask, dot(code, fold, 0, 1), 0.0).astype(bf16)

    ranked = jnp.concatenate(
        [
            rank_product(h, down_all, mask_fwd),
            rank_product(x, down_all, mask_back),
            rank_product(g, up_all, mask_back),
        ],
        axis=1,
    )
    ranked = summed(ranked, "mp")
    u = spread(ranked[:, :rows].astype(bf16), mask_fwd)
    ub = spread(ranked[:, rows : 2 * rows].astype(bf16), mask_back)
    v = spread((adapter_scale * ranked[:, 2 * rows :]).astype(bf16), mask_back)

    def factor_gradient(code, values, scale):
        own = dot(code[:, : held * rank], values, 0, 0)
        for k in range(1, owners):
            theirs = dot(code[:, k * held * rank : (k + 1) * held * rank], values, 0, 0)
            own = own + shifted(theirs.astype(bf16), "adapter", k).astype(f32)
        return (own * scale).astype(bf16).reshape(held, rank, width)

    grad_a = factor_gradient(v, x, 1.0 / seq_len)
    grad_b = factor_gradient(ub, g, adapter_scale / seq_len)

    lora = dot(u, up_all).astype(bf16).astype(f32)
    fwd_add = h.astype(f32) + adapter_scale * lora
    back_add = g.astype(f32) + dot(v, down_all).astype(bf16).astype(f32)
    if n <= longest_line:
        fwd_next, back_next = relay(h, g, weight, fwd_add, back_add, chunk_count)
    else:
        base = dot(lax.all_gather(h, "mp", axis=1, tiled=True), weight)
        terms = dot(g, weight, 1, 1).astype(bf16)
        back = lax.psum_scatter(terms, "mp", scatter_dimension=1, tiled=True).astype(f32)
        fwd_next = shifted((fwd_add + base).astype(bf16), "section", 1)
        back_next = shifted((back_add + back).astype(bf16), "section", -1)
    return (fwd_next[None], back_next[None], grad_a[None], grad_b[None])


def solution(mesh):
    in_specs = (
        P("section", "adapter", "mp"),
        P("section", "adapter", "mp"),
        P("section", "adapter", "mp"),
        P("section", None, "mp"),
        P("section", "adapter", None, "mp"),
        P("section", "adapter", None, "mp"),
        P(None, "section", "adapter"),
    )
    out_specs = (
        P("section", "adapter", "mp"),
        P("section", "adapter", "mp"),
        P("section", "adapter", None, "mp"),
        P("section", "adapter", None, "mp"),
    )
    return jax.shard_map(local, mesh=mesh, in_specs=in_specs, out_specs=out_specs, check_vma=False)
```

```python
import functools

import jax
import jax.numpy as jnp
from jax import lax
from jax.experimental import pallas as pl
from jax.experimental.pallas import tpu as pltpu
from jax.sharding import PartitionSpec as P

adapter_scale = 2.0
chunk_count = 4
longest_line = 4


def shifted(value, axis, steps):
    count = lax.axis_size(axis)
    pairs = [(source, (source + steps) % count) for source in range(count)]
    return lax.ppermute(value, axis, pairs)


def relay_kernel(
    n, chunks, h, g, weight, up_all, down_all, ranked, fold, mask_fwd, mask_back,
    fwd_next, back_next, codes, blocks, arrived, sending, results,
    gather_send, gather_recv, sum_send, sum_recv, relay_send, relay_recv, own_sem,
    rank_send, rank_recv, rank_parts, spread_fwd, spread_back,
):
    me = lax.axis_index("mp")
    section = lax.axis_index("section")
    sections = lax.axis_size("section")
    after = lax.rem(section + 1, sections)
    before = lax.rem(section + sections - 1, sections)
    rows, width = h.shape
    part = rows // chunks
    tile = min(512, width)
    narrow = min(256, width)
    mesh_id = pl.DeviceIdType.MESH

    def here(c):
        return pl.ds(pl.multiple_of(c * part, part), part)

    barrier = pltpu.get_barrier_semaphore()
    for other in (after, before):
        pl.semaphore_signal(barrier, 1, device_id={"section": other}, device_id_type=mesh_id)

    for step in range(1, n):
        peer = lax.rem(me + step, n)
        pl.semaphore_signal(barrier, 1, device_id={"mp": peer}, device_id_type=mesh_id)
    pl.semaphore_wait(barrier, n + 1)

    def rank_copy(step):
        return pltpu.make_async_remote_copy(
            src_ref=ranked,
            dst_ref=rank_parts.at[step - 1],
            send_sem=rank_send.at[step - 1],
            recv_sem=rank_recv.at[step - 1],
            device_id={"mp": lax.rem(me + step, n)},
            device_id_type=mesh_id,
        )

    for step in range(1, n):
        rank_copy(step).start()

    def sum_ranks():
        total = ranked[...].astype(jnp.float32)
        for step in range(1, n):
            rank_copy(step).wait_recv()
            total = total + rank_parts[step - 1].astype(jnp.float32)
        codes[:, : 2 * rows] = total[:, : 2 * rows].astype(jnp.bfloat16)
        codes[:, 2 * rows :] = (adapter_scale * total[:, 2 * rows :]).astype(jnp.bfloat16)

    def spread_into(out, first, mask, c):
        code = codes[:, pl.ds(pl.multiple_of(first * rows + c * part, part), part)]
        out[...] = (dot(code, fold[...], 0, 1) * mask[here(c), :]).astype(jnp.bfloat16)

    own = pltpu.make_async_copy(h, blocks.at[me], own_sem)
    own.start()

    def position(way):
        return me + way * (n - 1 - 2 * me)

    def toward(way):
        return me + 1 - 2 * way

    def gather_copy(way, t, c):
        block = me - (1 - 2 * way) * (t - 1)
        return pltpu.make_async_remote_copy(
            src_ref=h.at[here(c)] if isinstance(t, int) and t == 1 else blocks.at[block, here(c)],
            dst_ref=blocks.at[block, here(c)],
            send_sem=gather_send.at[way, t, c],
            recv_sem=gather_recv.at[way, t, c],
            device_id={"mp": toward(way)},
            device_id_type=mesh_id,
        )

    def gather_wait(way, t, c):
        block = me - (1 - 2 * way) * t
        pltpu.make_async_copy(
            blocks.at[block, here(c)], blocks.at[block, here(c)], gather_recv.at[way, t, c]
        ).wait()

    def sum_copy(way, t, c):
        block = me + (1 - 2 * way) * (n - t)
        return pltpu.make_async_remote_copy(
            src_ref=sending.at[block, here(c)],
            dst_ref=arrived.at[way, t, here(c)],
            send_sem=sum_send.at[way, t, c],
            recv_sem=sum_recv.at[way, t, c],
            device_id={"mp": toward(way)},
            device_id_type=mesh_id,
        )

    def sum_wait(way, t, c):
        pltpu.make_async_copy(
            arrived.at[way, t, here(c)], arrived.at[way, t, here(c)], sum_recv.at[way, t, c]
        ).wait()

    def relay_copy(which, c):
        return pltpu.make_async_remote_copy(
            src_ref=results.at[which, here(c)],
            dst_ref=(fwd_next, back_next)[which].at[here(c)],
            send_sem=relay_send.at[which, c],
            recv_sem=relay_recv.at[which, c],
            device_id={"section": (after, before)[which]},
            device_id_type=mesh_id,
        )

    def weight_rows(block):
        return weight.at[pl.ds(pl.multiple_of(block * width, width), width)]

    def product(block, c):
        return (
            [
                pl.BlockSpec((part, width), lambda j: (0, 0)),
                pl.BlockSpec((tile, width), lambda j: (j, 0)),
            ],
            [g.at[here(c)], weight_rows(block)],
        )

    piece = pl.BlockSpec((part, tile), lambda j: (0, j))

    def first_sum(block, c):
        def body(g_ref, w_ref, out_ref):
            out_ref[...] = dot(g_ref[...], w_ref[...], 1, 1).astype(jnp.bfloat16)

        specs, refs = product(block, c)
        pltpu.emit_pipeline(
            body, grid=(width // tile,), in_specs=specs, out_specs=[piece]
        )(*refs, sending.at[block, here(c)])

    def later_sum(way, t, block, c):
        def body(g_ref, w_ref, old_ref, out_ref):
            term = dot(g_ref[...], w_ref[...], 1, 1)
            out_ref[...] = (term + old_ref[...].astype(jnp.float32)).astype(jnp.bfloat16)

        specs, refs = product(block, c)
        pltpu.emit_pipeline(
            body, grid=(width // tile,), in_specs=specs + [piece], out_specs=[piece]
        )(*refs, arrived.at[way, t - 1, here(c)], sending.at[block, here(c)])

    def last_sum(c):
        spread_into(spread_back, 2, mask_back, c)

        def body(g_ref, w_ref, up_ref, down_ref, add_ref, table_ref, out_ref):
            total = dot(g_ref[...], w_ref[...], 1, 1) + add_ref[...].astype(jnp.float32)
            term = dot(spread_back[...], table_ref[...]).astype(jnp.bfloat16)
            total = total + term.astype(jnp.float32)
            up = jnp.where(me > 0, up_ref[...].astype(jnp.float32), 0.0)
            down = jnp.where(me < n - 1, down_ref[...].astype(jnp.float32), 0.0)
            out_ref[...] = (total + up + down).astype(jnp.bfloat16)

        specs, refs = product(me, c)
        table = pl.BlockSpec((down_all.shape[0], tile), lambda j: (0, j))
        pltpu.emit_pipeline(
            body, grid=(width // tile,), in_specs=specs + [piece] * 3 + [table], out_specs=[piece]
        )(
            *refs,
            arrived.at[0, n - 1, here(c)],
            arrived.at[1, n - 1, here(c)],
            g.at[here(c)],
            down_all,
            results.at[1, here(c)],
        )

    def base(c):
        spread_into(spread_fwd, 0, mask_fwd, c)

        def body(b_ref, w_ref, add_ref, table_ref, out_ref):
            term = dot(spread_fwd[...], table_ref[...]).astype(jnp.bfloat16)
            total = add_ref[...].astype(jnp.float32) + adapter_scale * term.astype(jnp.float32)
            for k in range(n):
                total = total + dot(b_ref[k], w_ref[k * width : (k + 1) * width, :])
            out_ref[...] = total.astype(jnp.bfloat16)

        strip = pl.BlockSpec((part, narrow), lambda j: (0, j))
        pltpu.emit_pipeline(
            body,
            grid=(width // narrow,),
            in_specs=[
                pl.BlockSpec((n, part, width), lambda j: (0, 0, 0)),
                pl.BlockSpec((n * width, narrow), lambda j: (0, j)),
                strip,
                pl.BlockSpec((up_all.shape[0], narrow), lambda j: (0, j)),
            ],
            out_specs=[strip],
        )(blocks.at[:, here(c)], weight, h.at[here(c)], up_all, results.at[0, here(c)])

    def start_gather(c):
        for way in range(2):
            @pl.when((c < chunks) & (position(way) < n - 1))
            def _():
                gather_copy(way, 1, c).start()

    start_gather(0)

    @pl.loop(0, chunks + n - 1)
    def _(slot):
        start_gather(slot + 1)

        @pl.loop(1, n)
        def _(t):
            c = slot - t + 1

            @pl.loop(0, 2)
            def _(way):
                place = position(way)

                @pl.when((c >= 0) & (c < chunks) & (place <= t - 1))
                def _():
                    block = me + (1 - 2 * way) * (n - t)

                    @pl.when(place == 0)
                    def _():
                        first_sum(block, c)

                    @pl.when(place > 0)
                    def _():
                        sum_wait(way, t - 1, c)
                        later_sum(way, t, block, c)

                    sum_copy(way, t, c).start()

                d = slot - t + 1

                @pl.when((d >= 0) & (d < chunks) & (place >= t))
                def _():
                    gather_wait(way, t, d)

                    @pl.when(place < n - 1)
                    def _():
                        gather_copy(way, t + 1, d).start()

        whole = slot - (n - 2)

        @pl.when(whole == 0)
        def _():
            own.wait()
            sum_ranks()

        @pl.when((whole >= 0) & (whole < chunks))
        def _():
            base(whole)
            relay_copy(0, whole).start()

        done = slot - (n - 1)

        @pl.when(done >= 0)
        def _():
            for way in range(2):
                @pl.when(position(way) > 0)
                def _():
                    sum_wait(way, n - 1, done)
            last_sum(done)
            relay_copy(1, done).start()

    for step in range(1, n):
        rank_copy(step).wait_send()

    @pl.loop(0, chunks)
    def _(c):
        for way in range(2):
            @pl.when(position(way) < n - 1)
            def _():
                gather_copy(way, 1, c).wait_send()

            @pl.loop(1, n)
            def _(t):
                @pl.when((position(way) < n - 1) & (position(way) >= t - 1) & (t > 1))
                def _():
                    gather_copy(way, t, c).wait_send()

                @pl.when(position(way) <= t - 1)
                def _():
                    sum_copy(way, t, c).wait_send()
            relay_copy(way, c).wait_send()
            relay_copy(way, c).wait_recv()


def relay(h, g, weight, up_all, down_all, ranked, fold, mask_fwd, mask_back, chunks):
    n = lax.axis_size("mp")
    rows, width = h.shape
    part = (rows, width)
    spread_shape = (rows // chunks, up_all.shape[0])
    shapes = [part, part, ranked.shape, (n,) + part, (2, n) + part, (n,) + part, (2,) + part]
    anywhere = pl.BlockSpec(memory_space=pl.ANY)
    inside = pl.BlockSpec(memory_space=pltpu.VMEM)
    dma = pltpu.SemaphoreType.DMA
    work = rows * weight.shape[0] * width * 4
    return pl.pallas_call(
        functools.partial(relay_kernel, n, chunks),
        out_shape=[jax.ShapeDtypeStruct(shape, jnp.bfloat16) for shape in shapes],
        in_specs=[anywhere] * 5 + [inside] * 4,
        out_specs=[anywhere] * 2 + [inside] + [anywhere] * 4,
        scratch_shapes=[
            dma((2, n, chunks)), dma((2, n, chunks)),
            dma((2, n, chunks)), dma((2, n, chunks)),
            dma((2, chunks)), dma((2, chunks)), dma,
            dma((n - 1,)), dma((n - 1,)),
            pltpu.VMEM((n - 1,) + ranked.shape, jnp.bfloat16),
            pltpu.VMEM(spread_shape, jnp.bfloat16),
            pltpu.VMEM(spread_shape, jnp.bfloat16),
        ],
        compiler_params=pltpu.CompilerParams(
            collective_id=0, has_side_effects=True, vmem_limit_bytes=56 * 2**20
        ),
        cost_estimate=pl.CostEstimate(flops=work, bytes_accessed=10**9, transcendentals=0),
    )(h, g, weight, up_all, down_all, ranked, fold, mask_fwd, mask_back)[:3]


def dot(a, b, a_dim=1, b_dim=0):
    return lax.dot_general(
        a, b, (((a_dim,), (b_dim,)), ((), ())), preferred_element_type=jnp.float32
    )


def local(
    forward_input,
    stored_input,
    output_gradient,
    frozen_weight,
    adapter_down_factor,
    adapter_up_factor,
    adapter_index_list,
):
    f32, bf16 = jnp.float32, jnp.bfloat16
    h, x, g = forward_input[0], stored_input[0], output_gradient[0]
    weight = frozen_weight[0]
    n = lax.axis_size("mp")
    owners = lax.axis_size("adapter")
    core = lax.axis_index("adapter")
    held, rank, width = adapter_down_factor.shape[1:]
    rows = h.shape[0]
    seq_count = adapter_index_list.shape[2]
    seq_len = rows // seq_count
    def all_tables(table):
        flat = table.reshape(held * rank, width)
        return jnp.concatenate(
            [flat] + [shifted(flat, "adapter", -k) for k in range(1, owners)], axis=0
        )

    down_all = all_tables(adapter_down_factor[0])
    up_all = all_tables(adapter_up_factor[0])
    total = owners * held
    columns = total * rank

    def mask_of(ids):
        place = (ids - core * held + total) % total
        token_place = jnp.repeat(place, seq_len)
        owner = lax.broadcasted_iota(jnp.int32, (rows, columns), 1) // rank
        return token_place[:, None] == owner

    mask_fwd = mask_of(adapter_index_list[0, 0])
    mask_back = mask_of(adapter_index_list[1, 0])
    fold = (
        lax.broadcasted_iota(jnp.int32, (columns, rank), 0) % rank
        == lax.broadcasted_iota(jnp.int32, (columns, rank), 1)
    ).astype(bf16)

    def rank_product(values, table, mask):
        product = jnp.where(mask, dot(values, table, 1, 1), 0.0).astype(bf16)
        return dot(fold, product, 0, 1)

    def spread(code, mask):
        return jnp.where(mask, dot(code, fold, 0, 1), 0.0).astype(bf16)

    ranked = jnp.concatenate(
        [
            rank_product(h, down_all, mask_fwd),
            rank_product(x, down_all, mask_back),
            rank_product(g, up_all, mask_back),
        ],
        axis=1,
    )
    if n <= longest_line:
        fwd_next, back_next, codes = relay(
            h, g, weight, up_all, down_all, ranked.astype(bf16), fold,
            mask_fwd.astype(bf16), mask_back.astype(bf16), chunk_count,
        )
    else:
        ranked = lax.psum(ranked, "mp")
        codes = jnp.concatenate(
            [ranked[:, : 2 * rows], adapter_scale * ranked[:, 2 * rows :]], axis=1
        ).astype(bf16)
    ub = spread(codes[:, rows : 2 * rows], mask_back)
    v = spread(codes[:, 2 * rows :], mask_back)

    def factor_gradient(code, values, scale):
        own = dot(code[:, : held * rank], values, 0, 0)
        for k in range(1, owners):
            theirs = dot(code[:, k * held * rank : (k + 1) * held * rank], values, 0, 0)
            own = own + shifted(theirs.astype(bf16), "adapter", k).astype(f32)
        return (own * scale).astype(bf16).reshape(held, rank, width)

    grad_a = factor_gradient(v, x, 1.0 / seq_len)
    grad_b = factor_gradient(ub, g, adapter_scale / seq_len)

    if n > longest_line:
        u = spread(codes[:, :rows], mask_fwd)
        lora = dot(u, up_all).astype(bf16).astype(f32)
        fwd_add = h.astype(f32) + adapter_scale * lora
        back_add = g.astype(f32) + dot(v, down_all).astype(bf16).astype(f32)
        base = dot(lax.all_gather(h, "mp", axis=1, tiled=True), weight)
        terms = dot(g, weight, 1, 1).astype(bf16)
        back = lax.psum_scatter(terms, "mp", scatter_dimension=1, tiled=True).astype(f32)
        fwd_next = shifted((fwd_add + base).astype(bf16), "section", 1)
        back_next = shifted((back_add + back).astype(bf16), "section", -1)
    return (fwd_next[None], back_next[None], grad_a[None], grad_b[None])


def solution(mesh):
    in_specs = (
        P("section", "adapter", "mp"),
        P("section", "adapter", "mp"),
        P("section", "adapter", "mp"),
        P("section", None, "mp"),
        P("section", "adapter", None, "mp"),
        P("section", "adapter", None, "mp"),
        P(None, "section", "adapter"),
    )
    out_specs = (
        P("section", "adapter", "mp"),
        P("section", "adapter", "mp"),
        P("section", "adapter", None, "mp"),
        P("section", "adapter", None, "mp"),
    )
    return jax.shard_map(local, mesh=mesh, in_specs=in_specs, out_specs=out_specs, check_vma=False)
```
